512 devices in a mesh: ctx: 64 (over z, y_hi, core), kvh: 8 (over y_lo, x).
Axes of the slice: x: 4, y: 8 (y_hi: 4, y_lo: 2; y = y_hi * 2 + y_lo), z: 8, core: 2. Of those that a mesh axis runs over, the one named last changes fastest.
Arguments:
- queries: bfloat16 [8192, 7168], P('ctx', 'kvh'), may hold values from -80 to 80
- keys: bfloat16 [8192, 1024], P('ctx', 'kvh'), may hold values from -4 to 4
- values: bfloat16 [8192, 1024], P('ctx', 'kvh'), may hold values from -6 to 6
- doc_ids: int32 [64], replicated, may hold values from 0 to 7, never falling along the last dimension, each value on 1 to 32 neighbouring positions
- query_pos: int32 [64], replicated, may hold values from 0 to 63, as said below
- selection: int32 [64, 64], replicated, may hold values 0 or 1
Outputs:
- attention: bfloat16 [8192, 7168], P(('ctx', 'kvh'))
- log_total: float32 [56, 8192], P('kvh', 'ctx')
The draws below stay inside these ranges and needn't reach their ends.
Inputs may be any that keep to these rules, and one draw needn't show every extreme that they name: `doc_ids`: never falling; each document covers 1 to 32 whole blocks, one exactly that many. `query_pos`: each block number once.
All inputs are finite; a program needn't handle non-finite values.
Results may differ from the reference program's by a relative error of at most 0.0044.
Values may be sent and summed in bfloat16 or wider, within the bound.
A program may use at most 128 MiB of HBM per device.

```python
import math
import jax
import jax.numpy as jnp
import numpy as np
from jax import lax

HEAD = 128
GROUP = 7
BLOCK = 128
KV_HEADS = 8
BLOCKS = 64
CTX = 8192


def shared_draw(key):
    order = jax.random.permutation(jax.random.fold_in(key, 11), BLOCKS).astype(jnp.int32)
    base = jnp.clip(jax.random.normal(jax.random.fold_in(key, 12), (CTX, KV_HEADS * HEAD), jnp.float32), -4.0, 4.0)
    return (order, base)


def draw_query_pos(key, part):
    order, base = shared_draw(key)
    return order


def draw_keys(key, part):
    order, base = shared_draw(key)
    return base.astype(jnp.bfloat16)


def draw_queries(key, part):
    key = jax.random.fold_in(key, 31)
    fresh = jnp.clip(jax.random.normal(key, (CTX, KV_HEADS * GROUP * HEAD), jnp.float32), -4.0, 4.0)
    return fresh.astype(jnp.bfloat16)


def set_ends(result, stream_key, smallest, high):
    longest = result.shape.index(max(result.shape))
    spots = []
    for shift in (0, 1):
        where = [jax.random.randint(jax.random.fold_in(stream_key, axis), (), 0, length) for axis, length in enumerate(result.shape)]
        where[longest] = (where[longest] + shift) % result.shape[longest]
        spots.append(tuple(where))
    return result.at[spots[0]].set(smallest).at[spots[1]].set(high)


def level_of(key, extent, shards, least, high):
    level, own = 1.0, jax.random.fold_in(key, 6)
    for dim, blocks in shards:
        heights = jnp.exp(jax.random.uniform(jax.random.fold_in(own, dim), (blocks,), jnp.float32, least / len(shards), high / len(shards)))
        level = level * jnp.repeat(heights, extent[dim] // blocks).reshape([-1 if axis == dim else 1 for axis in range(len(extent))])
    return level


def split_up(number_of, total, limit, skew):
    loads = [(1 << 20) // math.isqrt(standing ** skew) + 1 for standing in range(2, number_of + 1)]
    rest, counts = total - limit - (number_of - 1), [1] * (number_of - 1)
    while rest > 0:
        free = [i for i in range(number_of - 1) if counts[i] < limit]
        mass, budget = sum([loads[i] for i in free]), rest
        for i in free:
            addition = min(limit - counts[i], max(1, budget * loads[i] // mass), rest)
            counts[i] = counts[i] + addition
            rest = rest - addition
    return np.array([limit] + counts)


def uneven(rng, amount, total, reach, skew):
    if amount == 2:
        one = jax.random.randint(rng, (), max(1, total - reach), min(reach, total - 1) + 1)
        return jnp.stack([one, total - one])
    sizes = jnp.asarray(split_up(amount, total, reach, skew), jnp.int32)
    couples = (amount - 1) // 2
    donor, sink = sizes[1:1 + 2 * couples:2], sizes[2:2 + 2 * couples:2]
    room = jnp.minimum(donor - 1, reach - sink)
    moved = jax.random.randint(jax.random.fold_in(rng, 1), (couples,), 0, 1 << 20) % (room + 1)
    sizes = sizes.at[1:1 + 2 * couples:2].set(donor - moved).at[2:2 + 2 * couples:2].set(sink + moved)
    return sizes[jax.random.permutation(jax.random.fold_in(rng, 2), amount)]


def gaussian(rng, dims, width, limit, shards=(), kind=jnp.bfloat16):
    drawn = jax.random.normal(rng, dims, jnp.float32) * width
    if len(shards) > 0:
        drawn = level_of(rng, dims, shards, -0.22, 0.18) * drawn
    return jnp.clip(drawn, min=-limit, max=limit).astype(kind)


def setup_inputs(seed: int = 0) -> dict:
    key_of = jax.random.split(jax.random.key(seed), 7)
    queries = draw_queries(jax.random.fold_in(key_of[6], 71), 0)
    keys = draw_keys(jax.random.fold_in(key_of[6], 71), 0)
    values = gaussian(key_of[2], (CTX, KV_HEADS * HEAD), 1.0, 6.0, ((0, 64), (1, 8)))
    doc_ids = jnp.searchsorted(jnp.cumsum(uneven(key_of[3], BLOCKS // 8, BLOCKS, BLOCKS // 2, 2)), jnp.arange(BLOCKS), side="right").astype(jnp.int32)
    query_pos = draw_query_pos(jax.random.fold_in(key_of[6], 71), 0)
    selection = set_ends((jax.random.randint(key_of[5], (BLOCKS, BLOCKS), 0, 4) < 3).astype(jnp.int32), jax.random.fold_in(key_of[5], 1), 0, 1)
    return {"queries": queries, "keys": keys, "values": values, "doc_ids": doc_ids, "query_pos": query_pos, "selection": selection}


def reference(queries, keys, values, doc_ids, query_pos, selection):
    heads_kv = keys.shape[1] // HEAD
    inverse_root = HEAD ** -0.5
    window = (BLOCKS // 2) * BLOCK
    query_blocks = queries.reshape(BLOCKS, BLOCK, heads_kv, GROUP, HEAD)

    def attend_block(pair):
        block_rows, index = pair
        query_block = query_pos[index]
        first_key = jnp.clip((query_block + 1) * BLOCK - window, 0, CTX - window).astype(jnp.int32)
        key_rows = lax.dynamic_slice_in_dim(keys, first_key, window, 0).reshape(window, heads_kv, HEAD)
        value_rows = lax.dynamic_slice_in_dim(values, first_key, window, 0).reshape(window, heads_kv, HEAD)
        key_position = first_key + jnp.arange(window, dtype=jnp.int32)
        key_block = key_position // BLOCK
        query_position = query_block * BLOCK + jnp.arange(BLOCK, dtype=jnp.int32)
        same_doc = doc_ids[key_block] == doc_ids[query_block]
        chosen = (selection[query_block][key_block] == 1) | (key_block == query_block)
        allowed = (same_doc & chosen)[None, :] & (key_position[None, :] <= query_position[:, None])
        scores = jnp.einsum("qhgd,khd->hgqk", block_rows.astype(jnp.float32), key_rows.astype(jnp.float32)) * inverse_root
        masked = jnp.where(allowed, scores, jnp.float32(-1e30))
        row_top = jnp.max(masked, axis=-1)
        weights = jnp.where(allowed, jnp.exp(scores - row_top[..., None]), jnp.float32(0.0))
        total = jnp.sum(weights, axis=-1)
        rounded = lax.optimization_barrier(weights.astype(jnp.bfloat16))
        blended = jnp.einsum("hgqk,khd->qhgd", rounded.astype(jnp.float32), value_rows.astype(jnp.float32))
        blended = blended / jnp.transpose(total, (2, 0, 1))[..., None]
        return blended.astype(jnp.bfloat16).reshape(BLOCK, -1), row_top + jnp.log(total)

    outputs, logs = lax.map(attend_block, (query_blocks, jnp.arange(BLOCKS, dtype=jnp.int32)))
    attention = outputs.reshape(CTX, -1)
    log_total = jnp.transpose(logs, (1, 2, 0, 3)).reshape(heads_kv * GROUP, CTX)
    return attention, log_total
```

```python
import functools
import math

import jax
import jax.numpy as jnp
from jax import lax
from jax.experimental import pallas as pl
from jax.experimental.pallas import tpu as pltpu
from jax.sharding import PartitionSpec as P

HEAD = 128
BLOCK = 128
Z, Y = 8, 4
NEG = -1e30
PENALTY = 1e30
INV_ROOT = HEAD ** (-0.5)
SCALE2 = INV_ROOT * math.log2(math.e)
MESH = pl.DeviceIdType.MESH
BOTH = slice(None)

CHUNKS = (
    ((0, 0), (-1, 0), (1, 0), (0, 1)),
    ((0, 3), (-2, 0), (2, 0), (0, 2)),
    ((-1, 1), (1, 1), (-1, 3), (1, 3)),
    ((-3, 0), (3, 0), (-1, 2), (1, 2)),
    ((-2, 1), (2, 1), (-3, 1), (3, 1)),
    ((-3, 3), (3, 3), (-2, 3), (2, 3)),
    ((-2, 2), (2, 2), (4, 0), (4, 1)),
    ((4, 3), (-3, 2), (3, 2), (4, 2)),
)


def kernel(
    groups,
    ranks,
    docs,
    query_pos,
    selection,
    q_hbm,
    k_hbm,
    v_hbm,
    out,
    log_out,
    kv,
    q_in,
    v_in,
    q_t,
    m_ref,
    l_ref,
    acc,
    blended,
    in_sem,
    send_sem,
    near_sem,
    ring_sem,
    far_sem,
    sib_sem,
    a2a_send,
    a2a_recv,
    own_sem,
):
    me, head = lax.axis_index("ctx"), lax.axis_index("kvh")
    z, y, core = me // (2 * Y), (me // 2) % Y, me % 2

    def at(dz, dy, c=core):
        return (((z + dz + Z) % Z) * Y + (y + dy) % Y) * 2 + c

    up, down, sibling = at(1, 0), at(-1, 0), at(0, 0, 1 - core)
    y_next, y_last, y_far = at(0, 1), at(0, 3), at(0, 2)

    k_copy = pltpu.make_async_copy(k_hbm, kv.at[0, me], in_sem.at[0])
    v_copy = pltpu.make_async_copy(v_hbm, v_in, in_sem.at[1])
    q_copy = pltpu.make_async_copy(q_hbm, q_in, in_sem.at[2])
    k_copy.start()
    v_copy.start()
    q_copy.start()

    barrier = pltpu.get_barrier_semaphore()
    for peer in (up, down, y_next, y_last, y_far, sibling):
        pl.semaphore_signal(barrier, inc=1, device_id=(peer, head), device_id_type=MESH)
    for step in range(1, ranks):
        other = lax.rem(head + step, ranks)
        pl.semaphore_signal(barrier, inc=1, device_id=(me, other), device_id_type=MESH)
    v_copy.wait()
    kv[1, me] = v_in[...].T
    k_copy.wait()
    pl.semaphore_wait(barrier, 6 + ranks - 1)

    sent = []

    def describe(slot, part, target, recv):
        ref = kv.at[part, slot]
        return pltpu.make_async_remote_copy(
            src_ref=ref,
            dst_ref=ref,
            send_sem=send_sem.at[len(sent)],
            recv_sem=recv,
            device_id=(target, head),
            device_id_type=MESH,
        )

    def send(slot, part, target, recv):
        copy = describe(slot, part, target, recv)
        copy.start()
        sent.append(copy)

    def arrived(slot, part, recv):
        ref = kv.at[part, slot]
        pltpu.make_async_remote_copy(
            src_ref=ref,
            dst_ref=ref,
            send_sem=send_sem.at[0],
            recv_sem=recv,
            device_id=(sibling, head),
            device_id_type=MESH,
        ).wait_recv()

    def share(dz, dy):
        send(at(dz, dy), BOTH, sibling, sib_sem.at[(dz + Z) % Z, dy])

    def ring_send(side, step, dy):
        behind = -(step - 1) if side == 0 else step - 1
        part = side if step == 4 else BOTH
        send(at(behind, dy), part, (up, down)[side], ring_sem.at[side, step - 1, dy])

    def ring_take(step, dy, onward):
        for side in (0, 1):
            behind = -step if side == 0 else step
            part = side if step == 4 else BOTH
            arrived(at(behind, dy), part, ring_sem.at[side, step - 1, dy])
            if onward:
                ring_send(side, step + 1, dy)
            if step < 4:
                share(behind, dy)
        if step == 4:
            share(4, dy)

    def fan(dz):
        index = {-3: 0, 3: 1, 4: 2}[dz]
        send(at(dz, 0), BOTH, y_next, far_sem.at[index, 1])
        send(at(dz, 0), BOTH, y_last, far_sem.at[index, 0])

    def fan_take(dz):
        index = {-3: 0, 3: 1, 4: 2}[dz]
        for where, dy in ((0, 1), (1, 3)):
            arrived(at(dz, dy), BOTH, far_sem.at[index, where])
            share(dz, dy)

    block = query_pos[me]
    doc = docs[block]

    def penalty(slot):
        fine = (docs[slot] == doc) & (selection[block, slot] == 1) & (slot < block)
        return jnp.where(fine, jnp.float32(0.0), jnp.float32(PENALTY))

    def attend(pairs, last=False):
        slots = [at(dz, dy, 0) for dz, dy in pairs]
        pens = [(penalty(s), penalty(s + 1)) for s in slots]
        for dz, dy in pairs:
            arrived(at(dz, dy, 1 - core), BOTH, sib_sem.at[(dz + Z) % Z, dy])

        def one(g, carry):
            q = q_t[g]
            old = m_ref[g]
            top = old
            scores, values = [], []
            for slot, pen in zip(slots, pens):
                keys = kv[0, pl.ds(slot, 2)].reshape(2 * BLOCK, HEAD)
                s = jnp.dot(keys, q, preferred_element_type=jnp.float32)
                for half in (0, 1):
                    part = s[half * BLOCK : (half + 1) * BLOCK]
                    scores.append((part, pen[half]))
                    most = jnp.max(part.reshape(BLOCK // 8, 8, BLOCK), axis=0)
                    top = jnp.maximum(top, most - pen[half])
                    values.append(kv[1, slot + half])
            if last:
                part = jnp.dot(kv[0, block], q, preferred_element_type=jnp.float32)
                key = lax.broadcasted_iota(jnp.int32, (BLOCK, BLOCK), 0)
                query = lax.broadcasted_iota(jnp.int32, (BLOCK, BLOCK), 1)
                part = jnp.where(key <= query, part, jnp.float32(NEG))
                scores.append((part, jnp.float32(0.0)))
                top = jnp.maximum(top, jnp.max(part.reshape(BLOCK // 8, 8, BLOCK), axis=0))
                values.append(kv[1, block])
            new = jnp.max(top, axis=0, keepdims=True)
            keep = jnp.exp2((old - new) * SCALE2)
            total = l_ref[g] * keep
            weights = []
            for part, pen in scores:
                w = jnp.exp2((part - (new + 3.0 * pen)) * SCALE2)
                total = total + jnp.sum(w.reshape(BLOCK // 8, 8, BLOCK), axis=0)
                weights.append(w.astype(jnp.bfloat16))
            product = jnp.dot(
                jnp.concatenate(values, axis=1),
                jnp.concatenate(weights, axis=0),
                preferred_element_type=jnp.float32,
            )
            sums = acc[g] * keep[0:1] + product
            if last:
                whole = jnp.sum(total, axis=0, keepdims=True)
                ready = (sums / whole).T.astype(jnp.bfloat16)
                blended[:, pl.ds(pl.multiple_of(g * HEAD, HEAD), HEAD)] = ready
                log_out[pl.ds(g, 1), :] = new * INV_ROOT + jnp.log(whole)
            else:
                m_ref[g] = jnp.broadcast_to(new, (8, BLOCK))
                l_ref[g] = total
                acc[g] = sums
            return carry

        lax.fori_loop(0, groups, one, 0)

    ring_send(0, 1, 0)
    ring_send(1, 1, 0)
    send(me, BOTH, y_next, near_sem.at[1])
    send(me, BOTH, y_last, near_sem.at[0])
    share(0, 0)

    q_copy.wait()
    for g in range(groups):
        q_t[g] = q_in[:, g * HEAD : (g + 1) * HEAD].T
    m_ref[...] = jnp.full_like(m_ref, NEG)
    l_ref[...] = jnp.zeros_like(l_ref)
    acc[...] = jnp.zeros_like(acc)

    ring_take(1, 0, True)
    arrived(at(0, 1), BOTH, near_sem.at[0])
    send(at(0, 1), 1, y_last, near_sem.at[3])
    arrived(at(0, 3), BOTH, near_sem.at[1])
    send(at(0, 3), 0, y_next, near_sem.at[2])
    for dy in (1, 3):
        ring_send(0, 1, dy)
        ring_send(1, 1, dy)
        share(0, dy)
    ring_take(2, 0, True)
    attend(CHUNKS[0])
    arrived(at(0, 2), 0, near_sem.at[2])
    arrived(at(0, 2), 1, near_sem.at[3])
    ring_send(0, 1, 2)
    ring_send(1, 1, 2)
    share(0, 2)
    ring_take(1, 1, True)
    ring_take(3, 0, True)
    fan(-3)
    fan(3)
    attend(CHUNKS[1])
    ring_take(1, 3, True)
    ring_take(1, 2, True)
    attend(CHUNKS[2])
    ring_take(4, 0, False)
    fan(4)
    fan_take(-3)
    fan_take(3)
    attend(CHUNKS[3])
    ring_take(2, 2, True)
    ring_take(2, 1, False)
    attend(CHUNKS[4])
    ring_take(2, 3, False)
    fan_take(4)
    attend(CHUNKS[5])
    ring_take(3, 2, True)
    attend(CHUNKS[6])
    ring_take(4, 2, False)
    attend(CHUNKS[7], last=True)

    def strip(r):
        return pl.ds(pl.multiple_of(r * (BLOCK // ranks), BLOCK // ranks), BLOCK // ranks)

    width = groups * HEAD
    columns = pl.ds(pl.multiple_of(head * width, HEAD), width)
    moves = []
    for step in range(1, ranks):
        other = lax.rem(head + step, ranks)
        move = pltpu.make_async_remote_copy(
            src_ref=blended.at[strip(other), :],
            dst_ref=out.at[:, columns],
            send_sem=a2a_send.at[step],
            recv_sem=a2a_recv.at[step],
            device_id=(me, other),
            device_id_type=MESH,
        )
        move.start()
        moves.append(move)
    own = pltpu.make_async_copy(blended.at[strip(head), :], out.at[:, columns], own_sem)
    own.start()
    for copy in sent:
        copy.wait_send()
    for step, move in enumerate(moves, 1):
        source = lax.rem(head - step + ranks, ranks)
        there = pl.ds(pl.multiple_of(source * width, HEAD), width)
        pltpu.make_async_remote_copy(
            src_ref=blended.at[strip(head), :],
            dst_ref=out.at[:, there],
            send_sem=a2a_send.at[step],
            recv_sem=a2a_recv.at[step],
            device_id=(me, source),
            device_id_type=MESH,
        ).wait_recv()
        move.wait_send()
    own.wait()


SENDS = 32 + 2 * (4 + 4 + 2 + 2) + 4 + 6


def local(ranks, queries, keys, values, doc_ids, query_pos, selection):
    rows, width = queries.shape
    groups = width // HEAD
    dma = pltpu.SemaphoreType.DMA
    smem = pl.BlockSpec(memory_space=pltpu.SMEM)
    anywhere = pl.BlockSpec(memory_space=pl.ANY)
    return pl.pallas_call(
        functools.partial(kernel, groups, ranks),
        out_shape=(
            jax.ShapeDtypeStruct((rows // ranks, ranks * width), jnp.bfloat16),
            jax.ShapeDtypeStruct((groups, rows), jnp.float32),
        ),
        in_specs=[smem, smem, smem, anywhere, anywhere, anywhere],
        out_specs=(anywhere, pl.BlockSpec(memory_space=pltpu.VMEM)),
        scratch_shapes=[
            pltpu.VMEM((2, Z * Y * 2, BLOCK, HEAD), jnp.bfloat16),
            pltpu.VMEM((rows, width), jnp.bfloat16),
            pltpu.VMEM((BLOCK, HEAD), jnp.bfloat16),
            pltpu.VMEM((groups, HEAD, BLOCK), jnp.bfloat16),
            pltpu.VMEM((groups, 8, BLOCK), jnp.float32),
            pltpu.VMEM((groups, 8, BLOCK), jnp.float32),
            pltpu.VMEM((groups, HEAD, BLOCK), jnp.float32),
            pltpu.VMEM((rows, width), jnp.bfloat16),
            dma((3,)),
            dma((SENDS,)),
            dma((4,)),
            dma((2, 4, Y)),
            dma((3, 2)),
            dma((Z, Y)),
            dma((ranks,)),
            dma((ranks,)),
            dma,
        ],
        compiler_params=pltpu.CompilerParams(
            collective_id=0, has_side_effects=True, vmem_limit_bytes=32 * 1024 * 1024
        ),
        cost_estimate=pl.CostEstimate(
            flops=4 * rows * width * Z * Y * 2 * BLOCK,
            bytes_accessed=4 * rows * width,
            transcendentals=rows * groups * Z * Y * 2 * BLOCK,
        ),
    )(doc_ids, query_pos, selection, queries, keys, values)


def solution(mesh):
    in_specs = (P("ctx", "kvh"), P("ctx", "kvh"), P("ctx", "kvh"), P(), P(), P())
    out_specs = (P(("ctx", "kvh"), None), P("kvh", "ctx"))
    return jax.shard_map(
        functools.partial(local, mesh.shape["kvh"]),
        mesh=mesh,
        in_specs=in_specs,
        out_specs=out_specs,
        check_vma=False,
    )
```

```python
import functools
import math

import jax
import jax.numpy as jnp
from jax import lax
from jax.experimental import pallas as pl
from jax.experimental.pallas import tpu as pltpu
from jax.sharding import PartitionSpec as P

HEAD = 128
BLOCK = 128
Z, Y = 8, 4
NEG = -1e30
PENALTY = 1e30
INV_ROOT = HEAD ** (-0.5)
SCALE2 = INV_ROOT * math.log2(math.e)
MESH = pl.DeviceIdType.MESH
BOTH = slice(None)

WAY_NEXT = {1: "z", 2: "z", 3: "z", 4: "z"}
WAY_FAR = {1: "z", 2: "f", 3: "z", 4: "f"}
ORDER = ((1, 0), (0, 1), (0, 3), (2, 0), (1, 1), (0, 2), (1, 3), (3, 0), (2, 1), (1, 2), (2, 3), (4, 0), (2, 2), (3, 1), (3, 3), (3, 2), (4, 1), (4, 3), (4, 2))
LAG = 2
PER_CHUNK = 4


def way(d, dy):
    if d == 0:
        return "f"
    return "z" if dy == 0 else WAY_FAR[d] if dy == 2 else WAY_NEXT[d]


def rows_of(d):
    return (0,) if d == 0 else (4,) if d == 4 else (-d, d)


def program():
    steps, waiting, due = [], [(0, 0)], []
    for place, (d, dy) in enumerate(ORDER):
        steps.append(("take", d, dy))
        waiting += [(dz, dy) for dz in rows_of(d)]
        while len(waiting) >= PER_CHUNK:
            due.append((place + LAG, waiting[:PER_CHUNK]))
            waiting = waiting[PER_CHUNK:]
        while due and due[0][0] <= place and place < len(ORDER) - 1:
            steps.append(("attend", due.pop(0)[1], False))
    due = [pairs for _, pairs in due] + ([waiting] if waiting else [])
    return steps + [("attend", pairs, i == len(due) - 1) for i, pairs in enumerate(due)]


def kernel(
    groups,
    ranks,
    docs_hbm,
    pos_hbm,
    selection_hbm,
    q_hbm,
    k_hbm,
    v_hbm,
    out,
    log_out,
    kv,
    docs,
    query_pos,
    selection,
    q_in,
    v_in,
    scores,
    q_t,
    m_ref,
    l_ref,
    acc,
    blended,
    in_sem,
    send_sem,
    take_sem,
    sib_sem,
    a2a_send,
    a2a_recv,
    own_sem,
):
    me, head = lax.axis_index("ctx"), lax.axis_index("kvh")
    z, y, core = me // (2 * Y), (me // 2) % Y, me % 2

    def at(dz, dy, c=core):
        return (((z + dz + Z) % Z) * Y + (y + dy) % Y) * 2 + c

    up, down, sibling = at(1, 0), at(-1, 0), at(0, 0, 1 - core)
    y_next, y_last, y_far = at(0, 1), at(0, 3), at(0, 2)

    k_copy = pltpu.make_async_copy(k_hbm, kv.at[0, me], in_sem.at[0])
    v_copy = pltpu.make_async_copy(v_hbm, v_in, in_sem.at[1])
    q_copy = pltpu.make_async_copy(q_hbm, q_in, in_sem.at[2])
    scalars = [
        pltpu.make_async_copy(here, there, in_sem.at[3 + i])
        for i, (here, there) in enumerate(((docs_hbm, docs), (pos_hbm, query_pos), (selection_hbm, selection)))
    ]
    for copy in (v_copy, k_copy, *scalars, q_copy):
        copy.start()

    barrier = pltpu.get_barrier_semaphore()
    for peer in (up, down, y_next, y_last, y_far, sibling):
        pl.semaphore_signal(barrier, inc=1, device_id=(peer, head), device_id_type=MESH)
    for step in range(1, ranks):
        other = lax.rem(head + step, ranks)
        pl.semaphore_signal(barrier, inc=1, device_id=(me, other), device_id_type=MESH)
    v_copy.wait()
    kv[1, me] = v_in[...].T
    k_copy.wait()
    pl.semaphore_wait(barrier, 6 + ranks - 1)

    sent = []

    def describe(slot, part, target, recv):
        ref = kv.at[part, slot]
        return pltpu.make_async_remote_copy(
            src_ref=ref,
            dst_ref=ref,
            send_sem=send_sem.at[len(sent)],
            recv_sem=recv,
            device_id=(target, head),
            device_id_type=MESH,
        )

    def send(slot, part, target, recv):
        copy = describe(slot, part, target, recv)
        copy.start()
        sent.append(copy)

    def arrived(slot, part, recv):
        ref = kv.at[part, slot]
        pltpu.make_async_remote_copy(
            src_ref=ref,
            dst_ref=ref,
            send_sem=send_sem.at[0],
            recv_sem=recv,
            device_id=(sibling, head),
            device_id_type=MESH,
        ).wait_recv()

    def share(dz, dy):
        send(at(dz, dy), BOTH, sibling, sib_sem.at[(dz + Z) % Z, dy])

    def onward(d, dy):
        for side in (0, 1):
            if d < 4 and way(d + 1, dy) == "z":
                part = side if d == 3 else BOTH
                send(at(-d if side == 0 else d, dy), part, (up, down)[side], take_sem.at[side, d + 1, dy])
        for side, dz in enumerate(rows_of(d)):
            if dy == 0 and way(d, 1) == "f":
                send(at(dz, 0), BOTH, y_next, take_sem.at[side, d, 3])
                send(at(dz, 0), BOTH, y_last, take_sem.at[side, d, 1])
            if dy == 0 and way(d, 2) == "f":
                send(at(dz, 0), BOTH, y_far, take_sem.at[side, d, 2])
            share(dz, dy)

    def take(d, dy):
        if d == 4 and way(d, dy) == "z":
            for side in (0, 1):
                arrived(at(4, dy), side, take_sem.at[side, 4, dy])
        else:
            for side, dz in enumerate(rows_of(d)):
                arrived(at(dz, dy), BOTH, take_sem.at[side, d, dy])
        onward(d, dy)

    onward(0, 0)
    q_copy.wait()
    for g in range(groups):
        q_t[:, g * HEAD : (g + 1) * HEAD] = q_in[:, g * HEAD : (g + 1) * HEAD].T
    m_ref[...] = jnp.full_like(m_ref, NEG)
    l_ref[...] = jnp.zeros_like(l_ref)
    acc[...] = jnp.zeros_like(acc)
    for copy in scalars:
        copy.wait()
    block = query_pos[me]
    doc = docs[block]

    def strip(r):
        return pl.ds(pl.multiple_of(r * (BLOCK // ranks), BLOCK // ranks), BLOCK // ranks)

    moves = []

    def hand_out(batch, first, width):
        columns = pl.ds(pl.multiple_of(head * (groups * HEAD) + first, HEAD), width)
        for step in range(1, ranks):
            other = lax.rem(head + step, ranks)
            move = pltpu.make_async_remote_copy(
                src_ref=blended.at[strip(other), pl.ds(first, width)],
                dst_ref=out.at[:, columns],
                send_sem=a2a_send.at[batch, step],
                recv_sem=a2a_recv.at[batch, step],
                device_id=(me, other),
                device_id_type=MESH,
            )
            move.start()
            moves.append((move, batch, step, first, width))
        own = pltpu.make_async_copy(
            blended.at[strip(head), pl.ds(first, width)], out.at[:, columns], own_sem.at[batch]
        )
        own.start()
        moves.append((own, batch, 0, first, width))

    def penalty(slot):
        fine = (docs[slot] == doc) & (selection[block, slot] == 1) & (slot < block)
        return jnp.where(fine, jnp.float32(0.0), jnp.float32(PENALTY))

    def attend(pairs, last=False):
        slots = [at(dz, dy, 0) for dz, dy in pairs]
        pens = [(penalty(s), penalty(s + 1)) for s in slots]
        for dz, dy in pairs:
            arrived(at(dz, dy, 1 - core), BOTH, sib_sem.at[(dz + Z) % Z, dy])

        flat = [(slot + half, pen[half]) for slot, pen in zip(slots, pens) for half in (0, 1)]
        units = [(g, min(2, groups - g)) for g in range(0, groups, 2)]
        key = lax.broadcasted_iota(jnp.int32, (BLOCK, BLOCK), 0)
        query = lax.broadcasted_iota(jnp.int32, (BLOCK, BLOCK), 1)

        def lanes(u):
            g, n = units[u]
            return slice(g * HEAD, (g + n) * HEAD)

        def score(u):
            q, wide = q_t[:, lanes(u)], units[u][1] * HEAD
            for i, slot in enumerate(slots):
                keys = kv[0, pl.ds(slot, 2)].reshape(2 * BLOCK, HEAD)
                scores[u % 2, i * 2 * BLOCK : (i + 1) * 2 * BLOCK, :wide] = jnp.dot(
                    keys, q, preferred_element_type=jnp.float32
                )
            if last:
                part = jnp.dot(kv[0, block], q, preferred_element_type=jnp.float32)
                mask = jnp.concatenate([key <= query] * units[u][1], axis=1)
                end = len(flat) * BLOCK
                scores[u % 2, end : end + BLOCK, :wide] = jnp.where(mask, part, jnp.float32(NEG))

        def blend(u):
            wide = units[u][1] * HEAD
            here = lanes(u)
            parts = flat + ([(block, jnp.float32(0.0))] if last else [])
            old = m_ref[:, here]
            top = old
            for i, (_, pen) in enumerate(parts):
                part = scores[u % 2, i * BLOCK : (i + 1) * BLOCK, :wide]
                top = jnp.maximum(top, jnp.max(part.reshape(BLOCK // 8, 8, wide), axis=0) - pen)
            new = jnp.max(top, axis=0, keepdims=True)
            keep = jnp.exp2((old - new) * SCALE2)
            total = l_ref[:, here] * keep
            weights = []
            for i, (_, pen) in enumerate(parts):
                part = scores[u % 2, i * BLOCK : (i + 1) * BLOCK, :wide]
                w = jnp.exp2((part - (new + 3.0 * pen)) * SCALE2)
                total = total + jnp.sum(w.reshape(BLOCK // 8, 8, wide), axis=0)
                weights.append(w.astype(jnp.bfloat16))
            product = jnp.dot(
                jnp.concatenate([kv[1, slot] for slot, _ in parts], axis=1),
                jnp.concatenate(weights, axis=0),
                preferred_element_type=jnp.float32,
            )
            sums = acc[:, here] * keep[0:1] + product
            if not last:
                m_ref[:, here] = jnp.broadcast_to(new, (8, wide))
                l_ref[:, here] = total
                acc[:, here] = sums
                return
            whole = jnp.sum(total, axis=0, keepdims=True)
            ready = sums / whole
            logs = new * INV_ROOT + jnp.log(whole)
            for j in range(units[u][1]):
                g = units[u][0] + j
                blended[:, g * HEAD : (g + 1) * HEAD] = ready[:, j * HEAD : (j + 1) * HEAD].T.astype(jnp.bfloat16)
                log_out[g : g + 1, :] = logs[:, j * HEAD : (j + 1) * HEAD]

        score(0)
        sent_heads = 0
        for u in range(len(units)):
            if u < len(units) - 1:
                score(u + 1)
            blend(u)
            if last and (u % 2 == 1 or u == len(units) - 1):
                done = sum(units[u])
                hand_out(u // 2, sent_heads * HEAD, (done - sent_heads) * HEAD)
                sent_heads = done

    for kind, *what in program():
        if kind == "take":
            take(*what)
        else:
            attend(*what)

    for copy in sent:
        copy.wait_send()
    for move, batch, step, first, width in moves:
        if step == 0:
            move.wait()
            continue
        source = lax.rem(head - step + ranks, ranks)
        there = pl.ds(pl.multiple_of(source * (groups * HEAD) + first, HEAD), width)
        pltpu.make_async_remote_copy(
            src_ref=blended.at[strip(head), pl.ds(first, width)],
            dst_ref=out.at[:, there],
            send_sem=a2a_send.at[batch, step],
            recv_sem=a2a_recv.at[batch, step],
            device_id=(me, source),
            device_id_type=MESH,
        ).wait_recv()
        move.wait_send()


SENDS = 80


def local(ranks, queries, keys, values, doc_ids, query_pos, selection):
    rows, width = queries.shape
    groups = width // HEAD
    dma = pltpu.SemaphoreType.DMA
    hbm = pl.BlockSpec(memory_space=pltpu.HBM)
    return pl.pallas_call(
        functools.partial(kernel, groups, ranks),
        out_shape=(
            jax.ShapeDtypeStruct((rows // ranks, ranks * width), jnp.bfloat16),
            jax.ShapeDtypeStruct((groups, rows), jnp.float32),
        ),
        in_specs=[hbm] * 6,
        out_specs=(hbm, pl.BlockSpec(memory_space=pltpu.VMEM)),
        scratch_shapes=[
            pltpu.VMEM((2, Z * Y * 2, BLOCK, HEAD), jnp.bfloat16),
            pltpu.SMEM(doc_ids.shape, jnp.int32),
            pltpu.SMEM(query_pos.shape, jnp.int32),
            pltpu.SMEM(selection.shape, jnp.int32),
            pltpu.VMEM((rows, width), jnp.bfloat16),
            pltpu.VMEM((BLOCK, HEAD), jnp.bfloat16),
            pltpu.VMEM((2, (2 * PER_CHUNK + 1) * BLOCK, 2 * BLOCK), jnp.float32),
            pltpu.VMEM((HEAD, width), jnp.bfloat16),
            pltpu.VMEM((8, width), jnp.float32),
            pltpu.VMEM((8, width), jnp.float32),
            pltpu.VMEM((HEAD, width), jnp.float32),
            pltpu.VMEM((rows, width), jnp.bfloat16),
            dma((6,)),
            dma((SENDS,)),
            dma((2, 5, Y)),
            dma((Z, Y)),
            dma((2, ranks)),
            dma((2, ranks)),
            dma((2,)),
        ],
        compiler_params=pltpu.CompilerParams(
            collective_id=0, has_side_effects=True, vmem_limit_bytes=62 * 1024 * 1024
        ),
        cost_estimate=pl.CostEstimate(
            flops=4 * rows * width * Z * Y * 2 * BLOCK,
            bytes_accessed=4 * rows * width,
            transcendentals=rows * groups * Z * Y * 2 * BLOCK,
        ),
    )(doc_ids, query_pos, selection, queries, keys, values)


def solution(mesh):
    in_specs = (P("ctx", "kvh"), P("ctx", "kvh"), P("ctx", "kvh"), P(), P(), P())
    out_specs = (P(("ctx", "kvh"), None), P("kvh", "ctx"))
    return jax.shard_map(
        functools.partial(local, mesh.shape["kvh"]),
        mesh=mesh,
        in_specs=in_specs,
        out_specs=out_specs,
        check_vma=False,
    )
```

```python
import functools
import math

import jax
import jax.numpy as jnp
from jax import lax
from jax.experimental import pallas as pl
from jax.experimental.pallas import tpu as pltpu
from jax.sharding import PartitionSpec as P

HEAD = 128
BLOCK = 128
Z, Y = 8, 4
NEG = -1e30
PENALTY = 1e30
INV_ROOT = HEAD ** (-0.5)
SCALE2 = INV_ROOT * math.log2(math.e)
MESH = pl.DeviceIdType.MESH
BOTH = slice(None)

WAY_NEXT = {1: "z", 2: "z", 3: "z", 4: "z"}
WAY_FAR = {1: "z", 2: "f", 3: "z", 4: "f"}
ORDER = ((1, 0), (0, 1), (0, 3), (2, 0), (1, 1), (0, 2), (1, 3), (3, 0), (2, 1), (1, 2), (2, 3), (4, 0), (2, 2), (3, 1), (3, 3), (3, 2), (4, 1), (4, 3), (4, 2))
LAG = 2
PER_BATCH = 2
BATCHES = 2
SIZES = (4, 4, 4, 4, 4, 4, 4, 2, 2)
PER_CHUNK = max(SIZES)


PARTS = (0, 1)


def way(d, dy):
    if d == 0:
        return "f"
    return "z" if dy == 0 else WAY_FAR[d] if dy == 2 else WAY_NEXT[d]


def rows_of(d):
    return (0,) if d == 0 else (4,) if d == 4 else (-d, d)


def program():
    steps, waiting, due, sizes = [], [(0, 0)], [], list(SIZES)
    for place, (d, dy) in enumerate(ORDER):
        over = d == 4 and way(d, dy) == "z"
        for part in PARTS if not over else (0,):
            for side in (0,) if d == 0 or (d == 4 and not over) else (0, 1):
                steps.append(("take", side, d, dy, (0, 1)[side] if over else part))
        waiting += [(dz, dy) for dz in rows_of(d)]
        while sizes and len(waiting) >= sizes[0]:
            due.append((place + LAG, waiting[: sizes[0]]))
            waiting = waiting[sizes.pop(0) :]
        while due and due[0][0] <= place and place < len(ORDER) - 1:
            steps.append(("attend", due.pop(0)[1], False))
    due = [pairs for _, pairs in due]
    return steps + [("attend", pairs, i == len(due) - 1) for i, pairs in enumerate(due)]


def kernel(
    groups,
    ranks,
    docs_hbm,
    pos_hbm,
    selection_hbm,
    q_hbm,
    k_hbm,
    v_hbm,
    out,
    log_out,
    kv,
    docs,
    query_pos,
    selection,
    q_in,
    v_in,
    scores,
    q_t,
    m_ref,
    l_ref,
    acc,
    blended,
    in_sem,
    send_sem,
    take_sem,
    sib_sem,
    a2a_send,
    a2a_recv,
    own_sem,
    log_in,
    log_sem,
):
    me, head = lax.axis_index("ctx"), lax.axis_index("kvh")
    z, y, core = me // (2 * Y), (me // 2) % Y, me % 2

    def at(dz, dy, c=core):
        return (((z + dz + Z) % Z) * Y + (y + dy) % Y) * 2 + c

    up, down, sibling = at(1, 0), at(-1, 0), at(0, 0, 1 - core)
    y_next, y_last, y_far = at(0, 1), at(0, 3), at(0, 2)

    k_copy = pltpu.make_async_copy(k_hbm, kv.at[0, me], in_sem.at[0])
    v_copy = pltpu.make_async_copy(v_hbm, v_in, in_sem.at[1])
    q_copy = pltpu.make_async_copy(q_hbm, q_in, in_sem.at[2])
    scalars = [
        pltpu.make_async_copy(here, there, in_sem.at[3 + i])
        for i, (here, there) in enumerate(((docs_hbm, docs), (pos_hbm, query_pos), (selection_hbm, selection)))
    ]
    for copy in (v_copy, k_copy, *scalars, q_copy):
        copy.start()

    barrier = pltpu.get_barrier_semaphore()
    for peer in (up, down, y_next, y_last, y_far, sibling):
        pl.semaphore_signal(barrier, inc=1, device_id=(peer, head), device_id_type=MESH)
    for step in range(1, ranks):
        other = lax.rem(head + step, ranks)
        pl.semaphore_signal(barrier, inc=1, device_id=(me, other), device_id_type=MESH)
    pl.semaphore_wait(barrier, 6 + ranks - 1)

    sent = []

    def describe(slot, part, target, recv, origin):
        ref = kv.at[part, slot]
        return pltpu.make_async_remote_copy(
            src_ref=ref if origin is None else origin,
            dst_ref=ref,
            send_sem=send_sem.at[len(sent)],
            recv_sem=recv,
            device_id=(target, head),
            device_id_type=MESH,
        )

    def send(slot, part, target, recv, origin=None):
        copy = describe(slot, part, target, recv, origin)
        copy.start()
        sent.append(copy)

    def arrived(slot, part, recv):
        ref = kv.at[part, slot]
        pltpu.make_async_remote_copy(
            src_ref=ref,
            dst_ref=ref,
            send_sem=send_sem.at[0],
            recv_sem=recv,
            device_id=(sibling, head),
            device_id_type=MESH,
        ).wait_recv()

    def share(dz, dy):
        send(at(dz, dy), BOTH, sibling, sib_sem.at[(dz + Z) % Z, dy])

    def onward(side, d, dy, part):
        origin = k_hbm if (d, dy, part) == (0, 0, 0) else None
        dz = 0 if d == 0 else -d if side == 0 else d
        index = PARTS.index(part)
        if d < 4 and way(d + 1, dy) == "z":
            for s in (0, 1) if d == 0 else (side,):
                piece = part
                if d == 3:
                    if part != BOTH and part != s:
                        continue
                    piece = s
                    index = 0
                send(at(dz, dy), piece, (up, down)[s], take_sem.at[s, d + 1, dy, index], origin)
        index = PARTS.index(part)
        if dy == 0 and way(d, 1) == "f":
            send(at(dz, 0), part, y_next, take_sem.at[side, d, 3, index], origin)
            send(at(dz, 0), part, y_last, take_sem.at[side, d, 1, index], origin)
        if dy == 0 and way(d, 2) == "f":
            send(at(dz, 0), part, y_far, take_sem.at[side, d, 2, index], origin)
        if part == PARTS[-1]:
            share(dz, dy)

    def take(side, d, dy, part):
        over = d == 4 and way(d, dy) == "z"
        dz = 0 if d == 0 else -d if side == 0 else d
        arrived(at(dz, dy), part, take_sem.at[side, d, dy, 0 if over else PARTS.index(part)])
        if not over:
            onward(side, d, dy, part)
        elif side == 1:
            for piece in PARTS:
                onward(0, d, dy, piece)

    onward(0, 0, 0, 0)
    v_copy.wait()
    kv[1, me] = v_in[...].T
    k_copy.wait()
    onward(0, 0, 0, 1)
    q_copy.wait()
    for g in range(groups):
        q_t[:, g * HEAD : (g + 1) * HEAD] = q_in[:, g * HEAD : (g + 1) * HEAD].T
    m_ref[...] = jnp.full_like(m_ref, NEG)
    l_ref[...] = jnp.zeros_like(l_ref)
    acc[...] = jnp.zeros_like(acc)
    for copy in scalars:
        copy.wait()
    block = query_pos[me]
    doc = docs[block]

    def strip(r):
        return pl.ds(pl.multiple_of(r * (BLOCK // ranks), BLOCK // ranks), BLOCK // ranks)

    moves = []

    def hand_out(batch, first, width):
        columns = pl.ds(first, width)
        for step in range(1, ranks):
            other = lax.rem(head + step, ranks)
            move = pltpu.make_async_remote_copy(
                src_ref=blended.at[strip(other), pl.ds(first, width)],
                dst_ref=out.at[head, :, columns],
                send_sem=a2a_send.at[batch, step],
                recv_sem=a2a_recv.at[batch, step],
                device_id=(me, other),
                device_id_type=MESH,
            )
            move.start()
            moves.append((move, batch, step, first, width))
        own = pltpu.make_async_copy(
            blended.at[strip(head), pl.ds(first, width)], out.at[head, :, columns], own_sem.at[batch]
        )
        own.start()
        moves.append((own, batch, 0, first, width))

    def penalty(slot):
        fine = (docs[slot] == doc) & (selection[block, slot] == 1) & (slot < block)
        return jnp.where(fine, jnp.float32(0.0), jnp.float32(PENALTY))

    def attend(pairs, last=False):
        slots = [at(dz, dy, 0) for dz, dy in pairs]
        pens = [(penalty(s), penalty(s + 1)) for s in slots]
        for dz, dy in pairs:
            arrived(at(dz, dy, 1 - core), BOTH, sib_sem.at[(dz + Z) % Z, dy])

        flat = [(slot + half, pen[half]) for slot, pen in zip(slots, pens) for half in (0, 1)]
        units = [(g, min(2, groups - g)) for g in range(0, groups, 2)]
        key = lax.broadcasted_iota(jnp.int32, (BLOCK, BLOCK), 0)
        query = lax.broadcasted_iota(jnp.int32, (BLOCK, BLOCK), 1)

        def lanes(u):
            g, n = units[u]
            return slice(g * HEAD, (g + n) * HEAD)

        def score(u):
            q, wide = q_t[:, lanes(u)], units[u][1] * HEAD
            for i, slot in enumerate(slots):
                keys = kv[0, pl.ds(slot, 2)].reshape(2 * BLOCK, HEAD)
                scores[u % 2, i * 2 * BLOCK : (i + 1) * 2 * BLOCK, :wide] = jnp.dot(
                    keys, q, preferred_element_type=jnp.float32
                )
            if last:
                part = jnp.dot(kv[0, block], q, preferred_element_type=jnp.float32)
                mask = jnp.concatenate([key <= query] * units[u][1], axis=1)
                end = len(flat) * BLOCK
                scores[u % 2, end : end + BLOCK, :wide] = jnp.where(mask, part, jnp.float32(NEG))

        def blend(u):
            wide = units[u][1] * HEAD
            here = lanes(u)
            parts = flat + ([(block, jnp.float32(0.0))] if last else [])
            old = m_ref[:, here]
            top = old
            for i, (_, pen) in enumerate(parts):
                part = scores[u % 2, i * BLOCK : (i + 1) * BLOCK, :wide]
                top = jnp.maximum(top, jnp.max(part.reshape(BLOCK // 8, 8, wide), axis=0) - pen)
            new = jnp.max(top, axis=0, keepdims=True)
            keep = jnp.exp2((old - new) * SCALE2)
            total = l_ref[:, here] * keep
            weights = []
            for i, (_, pen) in enumerate(parts):
                part = scores[u % 2, i * BLOCK : (i + 1) * BLOCK, :wide]
                w = jnp.exp2((part - (new + 3.0 * pen)) * SCALE2)
                total = total + jnp.sum(w.reshape(BLOCK // 8, 8, wide), axis=0)
                weights.append(w.astype(jnp.bfloat16))
            product = jnp.dot(
                jnp.concatenate([kv[1, slot] for slot, _ in parts], axis=1),
                jnp.concatenate(weights, axis=0),
                preferred_element_type=jnp.float32,
            )
            sums = acc[:, here] * keep[0:1] + product
            if not last:
                m_ref[:, here] = jnp.broadcast_to(new, (8, wide))
                l_ref[:, here] = total
                acc[:, here] = sums
                return
            whole = jnp.sum(total, axis=0, keepdims=True)
            ready = sums / whole
            logs = new * INV_ROOT + jnp.log(whole)
            for j in range(units[u][1]):
                g = units[u][0] + j
                blended[:, g * HEAD : (g + 1) * HEAD] = ready[:, j * HEAD : (j + 1) * HEAD].T.astype(jnp.bfloat16)
                log_in[g : g + 1, :] = logs[:, j * HEAD : (j + 1) * HEAD]

        score(0)
        sent_heads = 0
        for u in range(len(units)):
            if u < len(units) - 1:
                score(u + 1)
            blend(u)
            if last and (u % PER_BATCH == PER_BATCH - 1 or u == len(units) - 1):
                done = sum(units[u])
                hand_out(u // PER_BATCH, sent_heads * HEAD, (done - sent_heads) * HEAD)
                sent_heads = done
        if last:
            pltpu.make_async_copy(log_in, log_out, log_sem).start()

    for kind, *what in program():
        if kind == "take":
            take(*what)
        else:
            attend(*what)

    for copy in sent:
        copy.wait_send()
    for move, batch, step, first, width in moves:
        if step == 0:
            move.wait()
            continue
        source = lax.rem(head - step + ranks, ranks)
        pltpu.make_async_remote_copy(
            src_ref=blended.at[strip(head), pl.ds(first, width)],
            dst_ref=out.at[source, :, pl.ds(first, width)],
            send_sem=a2a_send.at[batch, step],
            recv_sem=a2a_recv.at[batch, step],
            device_id=(me, source),
            device_id_type=MESH,
        ).wait_recv()
        move.wait_send()
    pltpu.make_async_copy(log_in, log_out, log_sem).wait()


SENDS = 160


def local(ranks, queries, keys, values, doc_ids, query_pos, selection):
    rows, width = queries.shape
    groups = width // HEAD
    dma = pltpu.SemaphoreType.DMA
    hbm = pl.BlockSpec(memory_space=pltpu.HBM)
    strips, logs = pl.pallas_call(
        functools.partial(kernel, groups, ranks),
        out_shape=(
            jax.ShapeDtypeStruct((ranks, rows // ranks, width), jnp.bfloat16),
            jax.ShapeDtypeStruct((groups, rows), jnp.float32),
        ),
        in_specs=[hbm] * 6,
        out_specs=(hbm, hbm),
        scratch_shapes=[
            pltpu.VMEM((2, Z * Y * 2, BLOCK, HEAD), jnp.bfloat16),
            pltpu.SMEM(doc_ids.shape, jnp.int32),
            pltpu.SMEM(query_pos.shape, jnp.int32),
            pltpu.SMEM(selection.shape, jnp.int32),
            pltpu.VMEM((rows, width), jnp.bfloat16),
            pltpu.VMEM((BLOCK, HEAD), jnp.bfloat16),
            pltpu.VMEM((2, (2 * PER_CHUNK + 1) * BLOCK, 2 * BLOCK), jnp.float32),
            pltpu.VMEM((HEAD, width), jnp.bfloat16),
            pltpu.VMEM((8, width), jnp.float32),
            pltpu.VMEM((8, width), jnp.float32),
            pltpu.VMEM((HEAD, width), jnp.float32),
            pltpu.VMEM((rows, width), jnp.bfloat16),
            dma((6,)),
            dma((SENDS,)),
            dma((2, 5, Y, 2)),
            dma((Z, Y)),
            dma((BATCHES, ranks)),
            dma((BATCHES, ranks)),
            dma((BATCHES,)),
            pltpu.VMEM((groups, rows), jnp.float32),
            dma,
        ],
        compiler_params=pltpu.CompilerParams(
            collective_id=0, has_side_effects=True, vmem_limit_bytes=62 * 1024 * 1024
        ),
        cost_estimate=pl.CostEstimate(
            flops=4 * rows * width * Z * Y * 2 * BLOCK,
            bytes_accessed=4 * rows * width,
            transcendentals=rows * groups * Z * Y * 2 * BLOCK,
        ),
    )(doc_ids, query_pos, selection, queries, keys, values)
    return jnp.transpose(strips, (1, 0, 2)).reshape(rows // ranks, ranks * width), logs


def solution(mesh):
    in_specs = (P("ctx", "kvh"), P("ctx", "kvh"), P("ctx", "kvh"), P(), P(), P())
    out_specs = (P(("ctx", "kvh"), None), P("kvh", "ctx"))
    return jax.shard_map(
        functools.partial(local, mesh.shape["kvh"]),
        mesh=mesh,
        in_specs=in_specs,
        out_specs=out_specs,
        check_vma=False,
    )
```

```python
import functools
import math

import jax
import jax.numpy as jnp
from jax import lax
from jax.experimental import pallas as pl
from jax.experimental.pallas import tpu as pltpu
from jax.sharding import PartitionSpec as P

HEAD = 128
BLOCK = 128
Z, Y = 8, 4
NEG = -1e30
PENALTY = 1e30
INV_ROOT = HEAD ** (-0.5)
SCALE2 = INV_ROOT * math.log2(math.e)
MESH = pl.DeviceIdType.MESH
BOTH = slice(None)

WAY_NEXT = {1: "z", 2: "z", 3: "z", 4: "z"}
WAY_FAR = {1: "z", 2: "f", 3: "z", 4: "f"}
ORDER = ((1, 0), (0, 1), (0, 3), (2, 0), (1, 1), (0, 2), (1, 3), (3, 0), (2, 1), (2, 3), (1, 2), (4, 0), (2, 2), (3, 1), (3, 3), (4, 1), (4, 3), (3, 2), (4, 2))
LAG = 2
PER_BATCH = 2
BATCHES = 2
SIZES = (4, 4, 4, 4, 4, 4, 4, 2, 2)
PER_CHUNK = max(SIZES)


PARTS = (0, 1)


def way(d, dy):
    if d == 0:
        return "f"
    return "z" if dy == 0 else WAY_FAR[d] if dy == 2 else WAY_NEXT[d]


def rows_of(d):
    return (0,) if d == 0 else (4,) if d == 4 else (-d, d)


def program():
    steps, waiting, due, sizes = [], [(0, 0)], [], list(SIZES)
    for place, (d, dy) in enumerate(ORDER):
        over = d == 4 and way(d, dy) == "z"
        for part in PARTS if not over else (0,):
            for side in (0,) if d == 0 or (d == 4 and not over) else (0, 1):
                steps.append(("take", side, d, dy, (0, 1)[side] if over else part))
        waiting += [(dz, dy) for dz in rows_of(d)]
        while sizes and len(waiting) >= sizes[0]:
            due.append((place + LAG, waiting[: sizes[0]]))
            waiting = waiting[sizes.pop(0) :]
        while due and due[0][0] <= place and place < len(ORDER) - 1:
            steps.append(("attend", due.pop(0)[1], False))
    due = [pairs for _, pairs in due]
    return steps + [("attend", pairs, i == len(due) - 1) for i, pairs in enumerate(due)]


def kernel(
    groups,
    ranks,
    docs_hbm,
    pos_hbm,
    selection_hbm,
    q_hbm,
    k_hbm,
    v_hbm,
    out,
    log_out,
    kv,
    docs,
    query_pos,
    selection,
    q_in,
    v_in,
    scores,
    q_t,
    m_ref,
    l_ref,
    acc,
    blended,
    in_sem,
    send_sem,
    take_sem,
    sib_sem,
    a2a_send,
    a2a_recv,
    own_sem,
    log_in,
    log_sem,
):
    me, head = lax.axis_index("ctx"), lax.axis_index("kvh")
    z, y, core = me // (2 * Y), (me // 2) % Y, me % 2

    def at(dz, dy, c=core):
        return (((z + dz + Z) % Z) * Y + (y + dy) % Y) * 2 + c

    up, down, sibling = at(1, 0), at(-1, 0), at(0, 0, 1 - core)
    y_next, y_last, y_far = at(0, 1), at(0, 3), at(0, 2)

    k_copy = pltpu.make_async_copy(k_hbm, kv.at[0, me], in_sem.at[0])
    v_copy = pltpu.make_async_copy(v_hbm, v_in, in_sem.at[1])
    q_copy = pltpu.make_async_copy(q_hbm, q_in, in_sem.at[2])
    scalars = [
        pltpu.make_async_copy(here, there, in_sem.at[3 + i])
        for i, (here, there) in enumerate(((docs_hbm, docs), (pos_hbm, query_pos), (selection_hbm, selection)))
    ]
    v_copy.start()
    k_copy.start()

    barrier = pltpu.get_barrier_semaphore()
    for peer in (up, down, y_next, y_last, y_far, sibling):
        pl.semaphore_signal(barrier, inc=1, device_id=(peer, head), device_id_type=MESH)
    for step in range(1, ranks):
        other = lax.rem(head + step, ranks)
        pl.semaphore_signal(barrier, inc=1, device_id=(me, other), device_id_type=MESH)
    for copy in (*scalars, q_copy):
        copy.start()
    pl.semaphore_wait(barrier, 6 + ranks - 1)

    sent = []

    def describe(slot, part, target, recv, origin):
        ref = kv.at[part, slot]
        return pltpu.make_async_remote_copy(
            src_ref=ref if origin is None else origin,
            dst_ref=ref,
            send_sem=send_sem.at[len(sent)],
            recv_sem=recv,
            device_id=(target, head),
            device_id_type=MESH,
        )

    def send(slot, part, target, recv, origin=None):
        copy = describe(slot, part, target, recv, origin)
        copy.start()
        sent.append(copy)

    def arrived(slot, part, recv):
        ref = kv.at[part, slot]
        pltpu.make_async_remote_copy(
            src_ref=ref,
            dst_ref=ref,
            send_sem=send_sem.at[0],
            recv_sem=recv,
            device_id=(sibling, head),
            device_id_type=MESH,
        ).wait_recv()

    def share(dz, dy):
        send(at(dz, dy), BOTH, sibling, sib_sem.at[(dz + Z) % Z, dy])

    def onward(side, d, dy, part):
        origin = k_hbm if (d, dy, part) == (0, 0, 0) else None
        dz = 0 if d == 0 else -d if side == 0 else d
        index = PARTS.index(part)
        if d < 4 and way(d + 1, dy) == "z":
            for s in (0, 1) if d == 0 else (side,):
                piece = part
                if d == 3:
                    if part != BOTH and part != s:
                        continue
                    piece = s
                    index = 0
                send(at(dz, dy), piece, (up, down)[s], take_sem.at[s, d + 1, dy, index], origin)
        index = PARTS.index(part)
        if dy == 0 and way(d, 1) == "f":
            send(at(dz, 0), part, y_next, take_sem.at[side, d, 3, index], origin)
            send(at(dz, 0), part, y_last, take_sem.at[side, d, 1, index], origin)
        if dy == 0 and way(d, 2) == "f":
            send(at(dz, 0), part, y_far, take_sem.at[side, d, 2, index], origin)
        if part == PARTS[-1]:
            share(dz, dy)

    def take(side, d, dy, part):
        over = d == 4 and way(d, dy) == "z"
        dz = 0 if d == 0 else -d if side == 0 else d
        arrived(at(dz, dy), part, take_sem.at[side, d, dy, 0 if over else PARTS.index(part)])
        if not over:
            onward(side, d, dy, part)
        elif side == 1:
            for piece in PARTS:
                onward(0, d, dy, piece)

    onward(0, 0, 0, 0)
    v_copy.wait()
    kv[1, me] = v_in[...].T
    k_copy.wait()
    onward(0, 0, 0, 1)
    q_copy.wait()
    for g in range(groups):
        q_t[:, g * HEAD : (g + 1) * HEAD] = q_in[:, g * HEAD : (g + 1) * HEAD].T
    m_ref[...] = jnp.full_like(m_ref, NEG)
    l_ref[...] = jnp.zeros_like(l_ref)
    acc[...] = jnp.zeros_like(acc)
    for copy in scalars:
        copy.wait()
    block = query_pos[me]
    doc = docs[block]

    def strip(r):
        return pl.ds(pl.multiple_of(r * (BLOCK // ranks), BLOCK // ranks), BLOCK // ranks)

    moves = []

    def hand_out(batch, first, width):
        columns = pl.ds(first, width)
        for step in range(1, ranks):
            other = lax.rem(head + step, ranks)
            move = pltpu.make_async_remote_copy(
                src_ref=blended.at[strip(other), pl.ds(first, width)],
                dst_ref=out.at[head, :, columns],
                send_sem=a2a_send.at[batch, step],
                recv_sem=a2a_recv.at[batch, step],
                device_id=(me, other),
                device_id_type=MESH,
            )
            move.start()
            moves.append((move, batch, step, first, width))
        own = pltpu.make_async_copy(
            blended.at[strip(head), pl.ds(first, width)], out.at[head, :, columns], own_sem.at[batch]
        )
        own.start()
        moves.append((own, batch, 0, first, width))

    def penalty(slot):
        fine = (docs[slot] == doc) & (selection[block, slot] == 1) & (slot < block)
        return jnp.where(fine, jnp.float32(0.0), jnp.float32(PENALTY))

    def attend(pairs, last=False):
        slots = [at(dz, dy, 0) for dz, dy in pairs]
        pens = [(penalty(s), penalty(s + 1)) for s in slots]
        for dz, dy in pairs:
            arrived(at(dz, dy, 1 - core), BOTH, sib_sem.at[(dz + Z) % Z, dy])

        flat = [(slot + half, pen[half]) for slot, pen in zip(slots, pens) for half in (0, 1)]
        units = [(g, min(2, groups - g)) for g in range(0, groups, 2)]
        key = lax.broadcasted_iota(jnp.int32, (BLOCK, BLOCK), 0)
        query = lax.broadcasted_iota(jnp.int32, (BLOCK, BLOCK), 1)

        def lanes(u):
            g, n = units[u]
            return slice(g * HEAD, (g + n) * HEAD)

        def score(u):
            q, wide = q_t[:, lanes(u)], units[u][1] * HEAD
            for i, slot in enumerate(slots):
                keys = kv[0, pl.ds(slot, 2)].reshape(2 * BLOCK, HEAD)
                scores[u % 2, i * 2 * BLOCK : (i + 1) * 2 * BLOCK, :wide] = jnp.dot(
                    keys, q, preferred_element_type=jnp.float32
                )
            if last:
                part = jnp.dot(kv[0, block], q, preferred_element_type=jnp.float32)
                mask = jnp.concatenate([key <= query] * units[u][1], axis=1)
                end = len(flat) * BLOCK
                scores[u % 2, end : end + BLOCK, :wide] = jnp.where(mask, part, jnp.float32(NEG))

        def blend(u):
            wide = units[u][1] * HEAD
            here = lanes(u)
            parts = flat + ([(block, jnp.float32(0.0))] if last else [])
            old = m_ref[:, here]
            top = old
            for i, (_, pen) in enumerate(parts):
                part = scores[u % 2, i * BLOCK : (i + 1) * BLOCK, :wide]
                top = jnp.maximum(top, jnp.max(part.reshape(BLOCK // 8, 8, wide), axis=0) - pen)
            new = jnp.max(top, axis=0, keepdims=True)
            keep = jnp.exp2((old - new) * SCALE2)
            total = l_ref[:, here] * keep
            weights = []
            for i, (_, pen) in enumerate(parts):
                part = scores[u % 2, i * BLOCK : (i + 1) * BLOCK, :wide]
                w = jnp.exp2((part - (new + 3.0 * pen)) * SCALE2)
                total = total + jnp.sum(w.reshape(BLOCK // 8, 8, wide), axis=0)
                weights.append(w.astype(jnp.bfloat16))
            product = jnp.dot(
                jnp.concatenate([kv[1, slot] for slot, _ in parts], axis=1),
                jnp.concatenate(weights, axis=0),
                preferred_element_type=jnp.float32,
            )
            sums = acc[:, here] * keep[0:1] + product
            if not last:
                m_ref[:, here] = jnp.broadcast_to(new, (8, wide))
                l_ref[:, here] = total
                acc[:, here] = sums
                return
            whole = jnp.sum(total, axis=0, keepdims=True)
            ready = sums / whole
            logs = new * INV_ROOT + jnp.log(whole)
            for j in range(units[u][1]):
                g = units[u][0] + j
                blended[:, g * HEAD : (g + 1) * HEAD] = ready[:, j * HEAD : (j + 1) * HEAD].T.astype(jnp.bfloat16)
                log_in[g : g + 1, :] = logs[:, j * HEAD : (j + 1) * HEAD]

        score(0)
        sent_heads = 0
        for u in range(len(units)):
            if u < len(units) - 1:
                score(u + 1)
            blend(u)
            if last and (u % PER_BATCH == PER_BATCH - 1 or u == len(units) - 1):
                done = sum(units[u])
                hand_out(u // PER_BATCH, sent_heads * HEAD, (done - sent_heads) * HEAD)
                sent_heads = done
        if last:
            pltpu.make_async_copy(log_in, log_out, log_sem).start()

    for kind, *what in program():
        if kind == "take":
            take(*what)
        else:
            attend(*what)

    for copy in sent:
        copy.wait_send()
    for move, batch, step, first, width in moves:
        if step == 0:
            move.wait()
            continue
        source = lax.rem(head - step + ranks, ranks)
        pltpu.make_async_remote_copy(
            src_ref=blended.at[strip(head), pl.ds(first, width)],
            dst_ref=out.at[source, :, pl.ds(first, width)],
            send_sem=a2a_send.at[batch, step],
            recv_sem=a2a_recv.at[batch, step],
            device_id=(me, source),
            device_id_type=MESH,
        ).wait_recv()
        move.wait_send()
    pltpu.make_async_copy(log_in, log_out, log_sem).wait()


SENDS = 160


def local(ranks, queries, keys, values, doc_ids, query_pos, selection):
    rows, width = queries.shape
    groups = width // HEAD
    dma = pltpu.SemaphoreType.DMA
    hbm = pl.BlockSpec(memory_space=pltpu.HBM)
    strips, logs = pl.pallas_call(
        functools.partial(kernel, groups, ranks),
        out_shape=(
            jax.ShapeDtypeStruct((ranks, rows // ranks, width), jnp.bfloat16),
            jax.ShapeDtypeStruct((groups, rows), jnp.float32),
        ),
        in_specs=[hbm] * 6,
        out_specs=(hbm, hbm),
        scratch_shapes=[
            pltpu.VMEM((2, Z * Y * 2, BLOCK, HEAD), jnp.bfloat16),
            pltpu.SMEM(doc_ids.shape, jnp.int32),
            pltpu.SMEM(query_pos.shape, jnp.int32),
            pltpu.SMEM(selection.shape, jnp.int32),
            pltpu.VMEM((rows, width), jnp.bfloat16),
            pltpu.VMEM((BLOCK, HEAD), jnp.bfloat16),
            pltpu.VMEM((2, (2 * PER_CHUNK + 1) * BLOCK, 2 * BLOCK), jnp.float32),
            pltpu.VMEM((HEAD, width), jnp.bfloat16),
            pltpu.VMEM((8, width), jnp.float32),
            pltpu.VMEM((8, width), jnp.float32),
            pltpu.VMEM((HEAD, width), jnp.float32),
            pltpu.VMEM((rows, width), jnp.bfloat16),
            dma((6,)),
            dma((SENDS,)),
            dma((2, 5, Y, 2)),
            dma((Z, Y)),
            dma((BATCHES, ranks)),
            dma((BATCHES, ranks)),
            dma((BATCHES,)),
            pltpu.VMEM((groups, rows), jnp.float32),
            dma,
        ],
        compiler_params=pltpu.CompilerParams(
            collective_id=0, has_side_effects=True, vmem_limit_bytes=62 * 1024 * 1024
        ),
        cost_estimate=pl.CostEstimate(
            flops=4 * rows * width * Z * Y * 2 * BLOCK,
            bytes_accessed=4 * rows * width,
            transcendentals=rows * groups * Z * Y * 2 * BLOCK,
        ),
    )(doc_ids, query_pos, selection, queries, keys, values)
    return jnp.transpose(strips, (1, 0, 2)).reshape(rows // ranks, ranks * width), logs


def solution(mesh):
    in_specs = (P("ctx", "kvh"), P("ctx", "kvh"), P("ctx", "kvh"), P(), P(), P())
    out_specs = (P(("ctx", "kvh"), None), P("kvh", "ctx"))
    return jax.shard_map(
        functools.partial(local, mesh.shape["kvh"]),
        mesh=mesh,
        in_specs=in_specs,
        out_specs=out_specs,
        check_vma=False,
    )
```
